512 devices in a mesh: row: 32 (over z, x_hi, core), col: 16 (over x_lo, y).
Axes of the slice: x: 4 (x_hi: 2, x_lo: 2; x = x_hi * 2 + x_lo), y: 8, z: 8, core: 2. Of those that a mesh axis runs over, the one named last changes fastest.
Arguments:
- tokens: bfloat16 [131072, 1024], P(('row', 'col')), may hold values from -6 to 6
- norm_gain: float32 [1024], replicated, may hold values from 0.1 to 1.9
- norm_shift: float32 [1024], replicated, may hold values from -3 to 3
- w_qkv: bfloat16 [1024, 1536], replicated, may hold values from -2 to 13
- links: int32 [512], P(('row', 'col')), may hold values from 0 to 511
Outputs:
- attended: float32 [131072, 512], P(('row', 'col'))
The draws below stay inside these ranges and needn't reach their ends.
All inputs are finite; a program needn't handle non-finite values.
Results may differ from the reference program's by a relative error of at most 0.014.
The reference program's roundings to bfloat16 on the way count: a program that leaves them out, or rounds other values in their place, can miss the bound.
Values may be sent and summed in bfloat16 or wider, within the bound.
No kernel may reach another device: no remote copies, remote signals or barrier semaphores. Data moves between devices by JAX's collectives and lax.ppermute only.
A program may use at most 128 MiB of HBM per device.

```python
import math
import jax
import jax.numpy as jnp
from jax import lax

D = 1024
HEADS = 8
HD = 64
BLOCK = 256
INNER = 512
BLOCKS = 512
TOKENS = 131072


def draw_w_qkv(key, part):
    first = jax.random.fold_in(key, 0)
    inner = HEADS * HD
    column = jnp.arange(3 * inner)
    spread = jnp.where(column < 2 * inner, 2.4, 1.0) / math.sqrt(D)
    base = jax.random.truncated_normal(first, -4.0, 4.0, (D, 3 * inner), jnp.float32)
    base = base * spread[None, :]
    return base.astype(jnp.bfloat16)


def with_ends(array, own_key, smallest, top_value):
    place = [jax.random.randint(jax.random.fold_in(own_key, axis), (), 0, length) for axis, length in enumerate(array.shape)]
    longest = array.shape.index(max(array.shape))
    beside = place[:longest] + [(place[longest] + 1) % array.shape[longest]] + place[longest + 1:]
    return array.at[tuple(place)].set(smallest).at[tuple(beside)].set(top_value)


def block_levels(rng, dims, cuts, least, largest):
    factor_of = 1.0
    for axis_at, shards_of in cuts:
        heights = jax.random.uniform(jax.random.fold_in(jax.random.fold_in(rng, 6), axis_at), (shards_of,), jnp.float32, least / len(cuts), largest / len(cuts))
        factor_of = factor_of * jnp.repeat(jnp.exp(heights), dims[axis_at] // shards_of).reshape((-1,) + (1,) * (len(dims) - 1 - axis_at))
    return factor_of


def gaussian(rng, dims, width, reach, cuts=(), kind=jnp.bfloat16):
    loudness = block_levels(rng, dims, cuts, -0.22, 0.18) if cuts else 1.0
    values = jax.random.normal(rng, dims, jnp.float32) * width * loudness
    return jnp.minimum(jnp.maximum(values, -reach), reach).astype(kind)


def setup_inputs(seed: int = 0) -> dict:
    arg_keys = jax.random.split(jax.random.key(seed), 6)
    tokens = gaussian(arg_keys[0], (TOKENS, D), 1.0, 6.0, ((0, 512),))
    norm_gain = jnp.clip(1.0 + 0.18 * jax.random.normal(arg_keys[1], (D,), jnp.float32), 0.1, 1.9)
    norm_shift = gaussian(arg_keys[2], (D,), 0.5, 3.0, (), jnp.float32)
    w_qkv = draw_w_qkv(jax.random.fold_in(arg_keys[5], 71), 0)
    links = with_ends(jax.random.randint(arg_keys[4], (BLOCKS,), 0, BLOCKS), jax.random.fold_in(arg_keys[4], 1), 0, BLOCKS - 1).astype(jnp.int32)
    return dict(tokens=tokens, norm_gain=norm_gain, norm_shift=norm_shift, w_qkv=w_qkv, links=links)


def layer_norm(tokens, norm_gain, norm_shift):
    values = tokens.astype(jnp.float32)
    row_mean = lax.optimization_barrier(jnp.mean(values, axis=-1, keepdims=True))
    centred = values - row_mean
    row_var = lax.optimization_barrier(jnp.mean(centred * centred, axis=-1, keepdims=True))
    return (centred * lax.rsqrt(row_var + 1e-05) * norm_gain + norm_shift).astype(jnp.bfloat16)

def attend_block(queries, keyval):
    query_heads = queries.astype(jnp.float32).reshape(BLOCK, HEADS, HD)
    key_heads = keyval[:, :INNER].astype(jnp.float32).reshape(BLOCK, HEADS, HD)
    value_heads = keyval[:, INNER:].astype(jnp.float32).reshape(BLOCK, HEADS, HD)
    scores = jnp.einsum('qhd,khd->hqk', query_heads, key_heads) * (1.0 / math.sqrt(HD))
    row_max = lax.optimization_barrier(jnp.max(scores, axis=-1))
    weights = jnp.exp(scores - row_max[:, :, None])
    row_sum = lax.optimization_barrier(jnp.sum(weights, axis=-1))
    rounded = lax.optimization_barrier(weights.astype(jnp.bfloat16)).astype(jnp.float32)
    partial_value = jnp.einsum('hqk,khd->qhd', rounded, value_heads).astype(jnp.bfloat16)
    return (lax.optimization_barrier(partial_value), row_max, row_sum)

def combine(results, valid_flags):
    valid = jnp.stack(valid_flags)[:, None, None]
    maxima = jnp.stack([entry[1] for entry in results])
    top = lax.optimization_barrier(jnp.max(jnp.where(valid, maxima, -jnp.inf), axis=0))
    factors = jnp.where(valid, jnp.exp(maxima - top[None]), 0.0)
    sums = lax.optimization_barrier(jnp.sum(factors * jnp.stack([entry[2] for entry in results]), axis=0))
    accum = jnp.zeros((BLOCK, HEADS, HD), jnp.float32)
    for index, entry in enumerate(results):
        accum = accum + factors[index].T[:, :, None] * entry[0].astype(jnp.float32)
    return (accum / sums.T[:, :, None]).reshape(BLOCK, HEADS * HD)

def reference(tokens, norm_gain, norm_shift, w_qkv, links):
    normed = layer_norm(tokens, norm_gain, norm_shift)
    projected = jnp.dot(normed, w_qkv, preferred_element_type=jnp.float32).astype(jnp.bfloat16)
    query_all = projected[:, :INNER]
    keyval_all = projected[:, INNER:]
    sections = BLOCKS.bit_length() - 1

    def one_block(block_id):
        neighbours = [block_id, block_id - 1, block_id + 1]
        valid_flags = [block_id >= 0, block_id > 0, block_id < BLOCKS - 1]
        for section in range(sections):
            neighbours.append(jnp.bitwise_xor(block_id, 1 << section))
            valid_flags.append(jnp.bitwise_and(jnp.right_shift(links[block_id], section), 1) == 1)
        queries = lax.dynamic_slice_in_dim(query_all, (block_id * BLOCK).astype(jnp.int32), BLOCK, 0)
        results = []
        for neighbour in neighbours:
            start = (jnp.clip(neighbour, 0, BLOCKS - 1) * BLOCK).astype(jnp.int32)
            keyval = lax.dynamic_slice_in_dim(keyval_all, start, BLOCK, 0)
            results.append(attend_block(queries, keyval))
        return combine(results, valid_flags)
    outputs = lax.map(one_block, jnp.arange(BLOCKS, dtype=jnp.int32))
    return outputs.reshape(TOKENS, INNER)
```

```python
import functools
import math

import jax
import jax.numpy as jnp
from jax import lax
from jax.experimental import pallas as pl
from jax.experimental.pallas import tpu as pltpu
from jax.sharding import PartitionSpec as P

AXES = ("row", "col")
HEADS = 8
HD = 64
BLOCK = 256
INNER = HEADS * HD
WIDE = 3 * HD
SLOTS = 2
KEYS = 4
CHUNK = SLOTS * WIDE + 16
BACK = HD + 16
LOW = -1e30
SCALE = 1.0 / math.sqrt(HD)
LOG2E = math.log2(math.e)
Y_COUNT = 8
CORE_BIT = 4
VMEM_LIMIT = 32 * 1024 * 1024


def fields(index):
    return index & 7, (index >> 3) & 1, (index >> 4) & 1, (index >> 5) & 1, index >> 6


def split_groups(count):
    groups = {}
    for index in range(count):
        y, x_lo, core, x_hi, z = fields(index)
        key = (0, z, x_hi, x_lo) if core == 0 else (1, y, x_hi, x_lo)
        groups.setdefault(key, []).append(index)
    return [groups[key] for key in sorted(groups)]


def xor_pairs(count, bit):
    return [(index, index ^ (1 << bit)) for index in range(count)]


def edge_pairs(count):
    pairs = []
    for index in range(count):
        y = index % Y_COUNT
        if y == Y_COUNT - 1 and index + 1 < count:
            pairs.append((index, index + 1))
        if y == 0 and index > 0:
            pairs.append((index, index - 1))
    return pairs


def normalize(tokens, gain, shift):
    values = tokens.astype(jnp.float32)
    centred = values - jnp.mean(values, axis=-1, keepdims=True)
    row_var = jnp.mean(centred * centred, axis=-1, keepdims=True)
    return (centred * lax.rsqrt(row_var + 1e-05) * gain + shift).astype(jnp.bfloat16)


def key_times(index, links, core):
    y = index & 7
    bits = [(links >> bit) & 1 for bit in range(9)]
    odd = y & 1
    before = jnp.where(y > 0, 1 + odd * bits[0], 0)
    after = jnp.where(y < Y_COUNT - 1, 1 + (1 - odd) * bits[0], 0)
    along_y = (before, after, bits[1], bits[2])
    along_z = (jnp.int32(1), bits[6], bits[7], bits[8])
    return [jnp.where(core == 0, one, two) for one, two in zip(along_y, along_z)]


def key_members(member, core):
    along_y = (jnp.maximum(member - 1, 0), jnp.minimum(member + 1, HEADS - 1), member ^ 2, member ^ 4)
    along_z = (member, member ^ 1, member ^ 2, member ^ 4)
    return [jnp.where(core == 0, one, two) for one, two in zip(along_y, along_z)]


def stack_rows(rows, width, kind=jnp.float32):
    line = lax.broadcasted_iota(jnp.int32, (16, width), 0)
    table = jnp.zeros((16, width), kind)
    for entry, row in enumerate(rows):
        table = jnp.where(line == entry, row, table)
    return table


def norm_kernel(index_ref, links_ref, tokens_hbm, gain_hbm, shift_hbm, out_ref, tokens_ref, gain_ref, shift_ref, sems):
    copies = [
        pltpu.make_async_copy(source, target, sems.at[at])
        for at, (source, target) in enumerate(
            ((tokens_hbm, tokens_ref), (gain_hbm, gain_ref), (shift_hbm, shift_ref))
        )
    ]
    for copy in copies:
        copy.start()
    index = index_ref[0]
    times = key_times(index, links_ref[0], 1 - ((index >> CORE_BIT) & 1))
    out_ref[BLOCK:, :] = stack_rows(times, out_ref.shape[1], jnp.int32).astype(jnp.float32).astype(jnp.bfloat16)
    for copy in copies:
        copy.wait()
    out_ref[:BLOCK, :] = normalize(tokens_ref[...], gain_ref[...], shift_ref[...])


def project_kernel(index_ref, links_ref, own_ref, other_ref, w_hbm, chunk_ref, keyval_ref, normed_ref, w_ref, sems):
    tile = 4 * HD
    parts = 3 * INNER // tile
    copies = []
    for part in range(parts):
        columns = pl.ds(part * tile, tile)
        copies.append(pltpu.make_async_copy(w_hbm.at[:, columns], w_ref.at[:, columns], sems.at[part]))
        copies[-1].start()
    index = index_ref[0]
    times = key_times(index, links_ref[0], (index >> CORE_BIT) & 1)
    table = stack_rows(times, BLOCK, jnp.int32).astype(jnp.float32)
    sent = other_ref[BLOCK:, :BLOCK].astype(jnp.float32)
    line = lax.broadcasted_iota(jnp.int32, (16, BLOCK), 0)
    for entry in range(KEYS):
        table = jnp.where(line == KEYS + entry, sent[entry : entry + 1], table)
    for head in range(HEADS):
        chunk_ref[head, SLOTS * WIDE :, :] = table.astype(jnp.bfloat16)
    normed_ref[:BLOCK] = own_ref[:BLOCK]
    normed_ref[BLOCK:] = other_ref[:BLOCK]
    for part in range(parts):
        copies[part].wait()
        product = jnp.dot(
            normed_ref[...], w_ref[:, part * tile : (part + 1) * tile], preferred_element_type=jnp.float32
        )
        turned = product.T.astype(jnp.bfloat16)
        kind = part * tile // INNER
        for local in range(4):
            head = (part * tile % INNER) // HD + local
            rows = turned[local * HD : (local + 1) * HD]
            for slot in range(SLOTS):
                start = slot * WIDE + kind * HD
                chunk_ref[head, start : start + HD, :] = rows[:, slot * BLOCK : (slot + 1) * BLOCK]
            if kind > 0:
                keyval_ref[head, (kind - 1) * HD : kind * HD, :] = rows[:, :BLOCK]


def attend_all(items, score_ref, weight_ref):
    for at, (query, key, _) in enumerate(items):
        score_ref[at] = lax.dot_general(key(), query(), (((0,), (0,)), ((), ())), preferred_element_type=jnp.float32)
    stats = []
    for at in range(len(items)):
        scores = score_ref[at]
        peak = jnp.max(scores, axis=0, keepdims=True)
        weights = jnp.exp2((scores - peak) * (SCALE * LOG2E))
        stats.append((peak * SCALE, jnp.sum(weights, axis=0, keepdims=True)))
        weight_ref[at] = weights.astype(jnp.bfloat16)
    return [
        (jnp.dot(value(), weight_ref[at], preferred_element_type=jnp.float32),) + stats[at]
        for at, (_, _, value) in enumerate(items)
    ]


def merge(items):
    maxima = [jnp.where(times > 0, peak, LOW) for _, peak, _, times in items]
    top = functools.reduce(jnp.maximum, maxima)
    accum = total = None
    for (value, _, row_sum, times), peak in zip(items, maxima):
        factor = times * jnp.exp2((peak - top) * LOG2E)
        value, row_sum = factor * value.astype(jnp.bfloat16).astype(jnp.float32), factor * row_sum
        accum = value if accum is None else accum + value
        total = row_sum if total is None else total + row_sum
    return accum, top, total


def thirds(value):
    high = value.astype(jnp.bfloat16).astype(jnp.float32)
    rest = value - high
    middle = rest.astype(jnp.bfloat16).astype(jnp.float32)
    return [high, middle, rest - middle]


def group_kernel(index_ref, held_ref, back_ref, score_ref, weight_ref):
    core = (index_ref[0] >> CORE_BIT) & 1

    def step(member, carry):
        table = held_ref[member, SLOTS * WIDE :, :].astype(jnp.float32)
        sources = key_members(member, core)
        load = lambda source, start: lambda: held_ref[source, start : start + HD, :]
        items = [
            (load(member, slot * WIDE), load(source, slot * WIDE + HD), load(source, slot * WIDE + 2 * HD))
            for slot in range(SLOTS)
            for source in sources
        ]
        results = attend_all(items, score_ref, weight_ref)
        for slot in range(SLOTS):
            at = slot * KEYS
            accum, top, total = merge(
                [results[at + entry] + (table[at + entry : at + entry + 1],) for entry in range(KEYS)]
            )
            start = slot * BACK
            back_ref[member, start : start + HD, :] = accum.astype(jnp.bfloat16)
            back_ref[member, start + HD : start + BACK, :] = stack_rows(thirds(top) + thirds(total), BLOCK).astype(
                jnp.bfloat16
            )
        return carry

    lax.fori_loop(0, HEADS, step, 0)


def home_kernel(index_ref, links_ref, chunk_ref, x_lo_ref, x_hi_ref, edge_ref, out_ref, score_ref, weight_ref, count):
    index = index_ref[0]
    y = index & 7
    outer = ((y == 0) & (index > 0)) | ((y == Y_COUNT - 1) & (index < count - 1))
    times = [(links_ref[0] >> bit) & 1 for bit in (4, 3, 5)] + [jnp.where(outer, 1, 0)]
    rows = [jnp.full((1, BLOCK), number, jnp.int32).astype(jnp.float32) for number in times]

    def step(pair, carry):
        items = []
        load = lambda ref, head, start: lambda: ref[head, start : start + HD, :]
        for head in (2 * pair, 2 * pair + 1):
            query = load(chunk_ref, head, 0)
            items.append((query, load(chunk_ref, head, WIDE + HD), load(chunk_ref, head, WIDE + 2 * HD)))
            for ref in (x_lo_ref, x_hi_ref, edge_ref):
                items.append((query, load(ref, head, 0), load(ref, head, HD)))
        results = attend_all(items, score_ref, weight_ref)
        for local in range(2):
            accum, top, total = merge([results[local * KEYS + entry] + (rows[entry],) for entry in range(KEYS)])
            head = 2 * pair + local
            out_ref[head, :HD, :] = accum
            out_ref[head, HD:, :] = stack_rows([top, total], BLOCK)[:8]
        return carry

    lax.fori_loop(0, HEADS // 2, step, 0)


def finish_kernel(home_ref, own_ref, other_ref, out_ref):
    for pair in range(HEADS // 2):
        turned = []
        for head in (2 * pair, 2 * pair + 1):
            parts = [(home_ref[head, :HD, :], home_ref[head, HD : HD + 1, :], home_ref[head, HD + 1 : HD + 2, :])]
            for ref, slot in ((own_ref, 0), (other_ref, 1)):
                base = slot * BACK
                value = ref[head, base : base + HD, :].astype(jnp.float32)
                stats = ref[head, base + HD : base + BACK, :].astype(jnp.float32)
                parts.append((value, stats[0:1] + stats[1:2] + stats[2:3], stats[3:4] + stats[4:5] + stats[5:6]))
            top = functools.reduce(jnp.maximum, [peak for _, peak, _ in parts])
            factors = [jnp.exp2((peak - top) * LOG2E) for _, peak, _ in parts]
            accum = sum(factor * value for factor, (value, _, _) in zip(factors, parts))
            total = sum(factor * row_sum for factor, (_, _, row_sum) in zip(factors, parts))
            turned.append(accum / total)
        out_ref[:, pair * 2 * HD : (pair + 1) * 2 * HD] = jnp.concatenate(turned, axis=0).T


SMEM = pl.BlockSpec(memory_space=pltpu.SMEM)
WHOLE = pl.BlockSpec(memory_space=pltpu.VMEM)
HBM = pl.BlockSpec(memory_space=pltpu.HBM)


def call(kernel, specs, shapes, scratch, flops, moved, *operands):
    return pl.pallas_call(
        kernel,
        in_specs=specs,
        out_specs=[WHOLE] * len(shapes) if isinstance(shapes, list) else WHOLE,
        out_shape=shapes,
        scratch_shapes=scratch,
        compiler_params=pltpu.CompilerParams(vmem_limit_bytes=VMEM_LIMIT),
        cost_estimate=pl.CostEstimate(flops=flops, bytes_accessed=moved, transcendentals=0),
    )(*operands)


def per_device(tokens, norm_gain, norm_shift, w_qkv, links, count):
    groups = split_groups(count)
    width = w_qkv.shape[0]
    bf16, f32 = jnp.bfloat16, jnp.float32
    index = (lax.axis_index("row") * lax.axis_size("col") + lax.axis_index("col")).astype(jnp.int32)[None]
    attend_scratch = [pltpu.VMEM((2 * KEYS, BLOCK, BLOCK), f32), pltpu.VMEM((2 * KEYS, BLOCK, BLOCK), bf16)]
    normed = call(
        norm_kernel,
        [SMEM] * 2 + [HBM] * 3,
        jax.ShapeDtypeStruct((BLOCK + 16, width), bf16),
        [
            pltpu.VMEM((BLOCK, width), bf16),
            pltpu.VMEM((1, width), f32),
            pltpu.VMEM((1, width), f32),
            pltpu.SemaphoreType.DMA((3,)),
        ],
        10**7,
        2**20,
        index,
        links,
        tokens,
        norm_gain[None, :],
        norm_shift[None, :],
    )
    other = lax.ppermute(normed, AXES, xor_pairs(count, CORE_BIT))
    chunks, keyval = call(
        project_kernel,
        [SMEM] * 2 + [WHOLE] * 2 + [HBM],
        [jax.ShapeDtypeStruct((HEADS, CHUNK, BLOCK), bf16), jax.ShapeDtypeStruct((HEADS, 2 * HD, BLOCK), bf16)],
        [pltpu.VMEM((2 * BLOCK, width), bf16), pltpu.VMEM(w_qkv.shape, bf16), pltpu.SemaphoreType.DMA((6,))],
        2 * 2 * BLOCK * w_qkv.shape[0] * w_qkv.shape[1],
        6 * 2**20,
        index,
        links,
        normed,
        other,
        w_qkv,
    )
    held = lax.all_to_all(chunks, AXES, 0, 0, axis_index_groups=groups, tiled=True)
    from_x_lo = lax.ppermute(keyval, AXES, xor_pairs(count, 3))
    from_x_hi = lax.ppermute(keyval, AXES, xor_pairs(count, 5))
    back = call(
        group_kernel,
        [SMEM, WHOLE],
        jax.ShapeDtypeStruct((HEADS, SLOTS * BACK, BLOCK), bf16),
        attend_scratch,
        64 * 4 * BLOCK * BLOCK * 256,
        3 * 2**20,
        index,
        held,
    )
    keyval, held = lax.optimization_barrier((keyval, held))
    from_edge = lax.ppermute(keyval, AXES, edge_pairs(count))
    back, from_x_lo, from_x_hi = lax.optimization_barrier((back, from_x_lo, from_x_hi))
    mine = lax.all_to_all(back, AXES, 0, 0, axis_index_groups=groups, tiled=True)
    home = call(
        functools.partial(home_kernel, count=count),
        [SMEM] * 2 + [WHOLE] * 4,
        jax.ShapeDtypeStruct((HEADS, HD + 8, BLOCK), f32),
        attend_scratch,
        32 * 4 * BLOCK * BLOCK * 256,
        4 * 2**20,
        index,
        links,
        chunks,
        from_x_lo,
        from_x_hi,
        from_edge,
    )
    theirs = lax.ppermute(mine, AXES, xor_pairs(count, CORE_BIT))
    return call(
        finish_kernel,
        [WHOLE] * 3,
        jax.ShapeDtypeStruct((BLOCK, INNER), f32),
        [],
        10**7,
        2 * 2**20,
        home,
        mine,
        theirs,
    )


def solution(mesh):
    placed = (P(AXES, None), P(), P(), P(), P(AXES))
    return jax.shard_map(
        functools.partial(per_device, count=mesh.size),
        mesh=mesh,
        in_specs=placed,
        out_specs=P(AXES, None),
        check_vma=False,
    )
```

```python
import functools
import math

import jax
import jax.numpy as jnp
from jax import lax
from jax.experimental import pallas as pl
from jax.experimental.pallas import tpu as pltpu
from jax.sharding import PartitionSpec as P

AXES = ("row", "col")
HEADS = 8
HD = 64
BLOCK = 256
INNER = HEADS * HD
WIDE = 3 * HD
SLOTS = 2
KEYS = 4
CHUNK = SLOTS * WIDE + 8
BACK = SLOTS * HD + 8
LOW = -1e30
SCALE = 1.0 / math.sqrt(HD)
LOG2E = math.log2(math.e)
Y_COUNT = 8
CORE_BIT = 4
VMEM_LIMIT = 32 * 1024 * 1024
WIDE_LIMIT = 56 * 1024 * 1024


def fields(index):
    return index & 7, (index >> 3) & 1, (index >> 4) & 1, (index >> 5) & 1, index >> 6


def split_groups(count):
    groups = {}
    for index in range(count):
        y, x_lo, core, x_hi, z = fields(index)
        key = (0, z, x_hi, x_lo) if core == 0 else (1, y, x_hi, x_lo)
        groups.setdefault(key, []).append(index)
    return [groups[key] for key in sorted(groups)]


def xor_pairs(count, bit):
    return [(index, index ^ (1 << bit)) for index in range(count)]


def edge_pairs(count):
    pairs = []
    for index in range(count):
        y = index % Y_COUNT
        if y == Y_COUNT - 1 and index + 1 < count:
            pairs.append((index, index + 1))
        if y == 0 and index > 0:
            pairs.append((index, index - 1))
    return pairs


def normalize(tokens, gain, shift):
    values = tokens.astype(jnp.float32)
    centred = values - jnp.mean(values, axis=-1, keepdims=True)
    row_var = jnp.mean(centred * centred, axis=-1, keepdims=True)
    return (centred * lax.rsqrt(row_var + 1e-05) * gain + shift).astype(jnp.bfloat16)


def key_times(index, links, core):
    y = index & 7
    bits = [(links >> bit) & 1 for bit in range(9)]
    odd = y & 1
    before = jnp.where(y > 0, 1 + odd * bits[0], 0)
    after = jnp.where(y < Y_COUNT - 1, 1 + (1 - odd) * bits[0], 0)
    along_y = (before, after, bits[1], bits[2])
    along_z = (jnp.int32(1), bits[6], bits[7], bits[8])
    return [jnp.where(core == 0, one, two) for one, two in zip(along_y, along_z)]


def key_members(member, core):
    along_y = (jnp.maximum(member - 1, 0), jnp.minimum(member + 1, HEADS - 1), member ^ 2, member ^ 4)
    along_z = (member, member ^ 1, member ^ 2, member ^ 4)
    return [jnp.where(core == 0, one, two) for one, two in zip(along_y, along_z)]


def stack_rows(rows, height, width, kind=jnp.float32):
    line = lax.broadcasted_iota(jnp.int32, (height, width), 0)
    table = jnp.zeros((height, width), kind)
    for entry, row in enumerate(rows):
        table = jnp.where(line == entry, row, table)
    return table


def norm_kernel(index_ref, links_ref, tokens_hbm, gain_hbm, shift_hbm, out_ref, tokens_ref, gain_ref, shift_ref, sems):
    copies = [
        pltpu.make_async_copy(source, target, sems.at[at])
        for at, (source, target) in enumerate(
            ((tokens_hbm, tokens_ref), (gain_hbm, gain_ref), (shift_hbm, shift_ref))
        )
    ]
    for copy in copies:
        copy.start()
    index = index_ref[0]
    times = key_times(index, links_ref[0], 1 - ((index >> CORE_BIT) & 1))
    out_ref[BLOCK:, :] = stack_rows(times, 16, out_ref.shape[1], jnp.int32).astype(jnp.float32).astype(jnp.bfloat16)
    for copy in copies:
        copy.wait()
    out_ref[:BLOCK, :] = normalize(tokens_ref[...], gain_ref[...], shift_ref[...])


def project(normed_ref, w_ref, kinds, store):
    tile = 4 * HD
    for kind in kinds:
        for start in range(0, INNER, tile):
            columns = w_ref[:, kind * INNER + start : kind * INNER + start + tile]
            product = jnp.dot(normed_ref[...], columns, preferred_element_type=jnp.float32)
            turned = product.T.astype(jnp.bfloat16)
            for local in range(4):
                store(kind, start // HD + local, turned[local * HD : (local + 1) * HD])


def project_kernel(index_ref, links_ref, own_ref, other_ref, w_ref, chunk_ref, keyval_ref, normed_ref):
    index = index_ref[0]
    times = key_times(index, links_ref[0], (index >> CORE_BIT) & 1)
    table = stack_rows(times, 8, BLOCK, jnp.int32).astype(jnp.float32)
    sent = other_ref[BLOCK:, :BLOCK].astype(jnp.float32)
    line = lax.broadcasted_iota(jnp.int32, (8, BLOCK), 0)
    for entry in range(KEYS):
        table = jnp.where(line == KEYS + entry, sent[entry : entry + 1], table)
    for head in range(HEADS):
        chunk_ref[head, SLOTS * WIDE :, :] = table.astype(jnp.bfloat16)
    normed_ref[:BLOCK] = own_ref[:BLOCK]
    normed_ref[BLOCK:] = other_ref[:BLOCK]

    def store(kind, head, rows):
        for slot in range(SLOTS):
            start = slot * WIDE + kind * HD
            chunk_ref[head, start : start + HD, :] = rows[:, slot * BLOCK : (slot + 1) * BLOCK]
        if kind > 0:
            keyval_ref[head, (kind - 1) * HD : kind * HD, :] = rows[:, :BLOCK]

    project(normed_ref, w_ref, (0, 1, 2), store)


def edge_kernel(normed_ref, w_ref, keyval_ref):
    def store(kind, head, rows):
        keyval_ref[head, (kind - 1) * HD : kind * HD, :] = rows

    project(normed_ref.at[pl.ds(0, BLOCK)], w_ref, (1, 2), store)


def attend_all(items, score_ref, weight_ref):
    for at, (query, key, _) in enumerate(items):
        score_ref[at] = lax.dot_general(key(), query(), (((0,), (0,)), ((), ())), preferred_element_type=jnp.float32)
    stats = []
    for at in range(len(items)):
        scores = score_ref[at]
        peak = jnp.max(scores, axis=0, keepdims=True)
        weights = jnp.exp2((scores - peak) * (SCALE * LOG2E))
        stats.append((peak * SCALE, jnp.sum(weights, axis=0, keepdims=True)))
        weight_ref[at] = weights.astype(jnp.bfloat16)
    return [
        (jnp.dot(value(), weight_ref[at], preferred_element_type=jnp.float32),) + stats[at]
        for at, (_, _, value) in enumerate(items)
    ]


def merge(items):
    maxima = [jnp.where(times > 0, peak, LOW) for _, peak, _, times in items]
    top = functools.reduce(jnp.maximum, maxima)
    accum = total = None
    for (value, _, row_sum, times), peak in zip(items, maxima):
        factor = times * jnp.exp2((peak - top) * LOG2E)
        value, row_sum = factor * value.astype(jnp.bfloat16).astype(jnp.float32), factor * row_sum
        accum = value if accum is None else accum + value
        total = row_sum if total is None else total + row_sum
    return accum, top, total


def thirds(value):
    high = value.astype(jnp.bfloat16).astype(jnp.float32)
    rest = value - high
    middle = rest.astype(jnp.bfloat16).astype(jnp.float32)
    return [high, middle, rest - middle]


def group_kernel(index_ref, held_ref, back_ref, score_ref, weight_ref):
    core = (index_ref[0] >> CORE_BIT) & 1

    def step(member, carry):
        table = held_ref[member, SLOTS * WIDE :, :].astype(jnp.float32)
        sources = key_members(member, core)
        load = lambda source, start: lambda: held_ref[source, start : start + HD, :]
        items = [
            (load(member, slot * WIDE), load(source, slot * WIDE + HD), load(source, slot * WIDE + 2 * HD))
            for slot in range(SLOTS)
            for source in sources
        ]
        results = attend_all(items, score_ref, weight_ref)
        stats = []
        for slot in range(SLOTS):
            at = slot * KEYS
            accum, top, total = merge(
                [results[at + entry] + (table[at + entry : at + entry + 1],) for entry in range(KEYS)]
            )
            back_ref[member, slot * HD : (slot + 1) * HD, :] = (accum / total).astype(jnp.bfloat16)
            stats.extend(thirds(top + jnp.log(total)))
        back_ref[member, SLOTS * HD :, :] = stack_rows(stats, 8, BLOCK).astype(jnp.bfloat16)
        return carry

    lax.fori_loop(0, HEADS, step, 0)


def home_kernel(index_ref, links_ref, chunk_ref, x_lo_ref, x_hi_ref, edge_ref, out_ref, score_ref, weight_ref, count):
    index = index_ref[0]
    y = index & 7
    outer = ((y == 0) & (index > 0)) | ((y == Y_COUNT - 1) & (index < count - 1))
    times = [(links_ref[0] >> bit) & 1 for bit in (4, 3, 5)] + [jnp.where(outer, 1, 0)]
    rows = [jnp.full((1, BLOCK), number, jnp.int32).astype(jnp.float32) for number in times]

    def step(pair, carry):
        items = []
        load = lambda ref, head, start: lambda: ref[head, start : start + HD, :]
        for head in (2 * pair, 2 * pair + 1):
            query = load(chunk_ref, head, 0)
            items.append((query, load(chunk_ref, head, WIDE + HD), load(chunk_ref, head, WIDE + 2 * HD)))
            for ref in (x_lo_ref, x_hi_ref, edge_ref):
                items.append((query, load(ref, head, 0), load(ref, head, HD)))
        results = attend_all(items, score_ref, weight_ref)
        for local in range(2):
            accum, top, total = merge([results[local * KEYS + entry] + (rows[entry],) for entry in range(KEYS)])
            head = 2 * pair + local
            out_ref[head, :HD, :] = accum
            out_ref[head, HD:, :] = stack_rows([top, total], 8, BLOCK)
        return carry

    lax.fori_loop(0, HEADS // 2, step, 0)


def finish_kernel(home_ref, own_ref, other_ref, out_ref):
    for pair in range(HEADS // 2):
        turned = []
        for head in (2 * pair, 2 * pair + 1):
            home_top = home_ref[head, HD : HD + 1, :]
            parts = [(home_ref[head, :HD, :], home_top, home_ref[head, HD + 1 : HD + 2, :])]
            for ref, slot in ((own_ref, 0), (other_ref, 1)):
                value = ref[head, slot * HD : (slot + 1) * HD, :].astype(jnp.float32)
                stats = ref[head, SLOTS * HD :, :].astype(jnp.float32)
                at = 3 * slot
                parts.append((value, stats[at : at + 1] + stats[at + 1 : at + 2] + stats[at + 2 : at + 3], 1.0))
            top = functools.reduce(jnp.maximum, [peak for _, peak, _ in parts])
            factors = [jnp.exp2((peak - top) * LOG2E) for _, peak, _ in parts]
            accum = sum(factor * value for factor, (value, _, _) in zip(factors, parts))
            total = sum(factor * row_sum for factor, (_, _, row_sum) in zip(factors, parts))
            turned.append(accum / total)
        out_ref[:, pair * 2 * HD : (pair + 1) * 2 * HD] = jnp.concatenate(turned, axis=0).T


SMEM = pl.BlockSpec(memory_space=pltpu.SMEM)
WHOLE = pl.BlockSpec(memory_space=pltpu.VMEM)
HBM = pl.BlockSpec(memory_space=pltpu.HBM)


def call(kernel, specs, shapes, scratch, flops, moved, *operands, limit=VMEM_LIMIT):
    return pl.pallas_call(
        kernel,
        in_specs=specs,
        out_specs=[WHOLE] * len(shapes) if isinstance(shapes, list) else WHOLE,
        out_shape=shapes,
        scratch_shapes=scratch,
        compiler_params=pltpu.CompilerParams(vmem_limit_bytes=limit),
        cost_estimate=pl.CostEstimate(flops=flops, bytes_accessed=moved, transcendentals=0),
    )(*operands)


def per_device(tokens, norm_gain, norm_shift, w_qkv, links, count):
    groups = split_groups(count)
    width = w_qkv.shape[0]
    bf16, f32 = jnp.bfloat16, jnp.float32
    index = (lax.axis_index("row") * lax.axis_size("col") + lax.axis_index("col")).astype(jnp.int32)[None]
    attend_scratch = [pltpu.VMEM((2 * KEYS, BLOCK, BLOCK), f32), pltpu.VMEM((2 * KEYS, BLOCK, BLOCK), bf16)]
    normed = call(
        norm_kernel,
        [SMEM] * 2 + [HBM] * 3,
        jax.ShapeDtypeStruct((BLOCK + 16, width), bf16),
        [
            pltpu.VMEM((BLOCK, width), bf16),
            pltpu.VMEM((1, width), f32),
            pltpu.VMEM((1, width), f32),
            pltpu.SemaphoreType.DMA((3,)),
        ],
        13 * 10**9,
        2**20,
        index,
        links,
        tokens,
        norm_gain[None, :],
        norm_shift[None, :],
        limit=WIDE_LIMIT,
    )
    other = lax.ppermute(normed, AXES, xor_pairs(count, CORE_BIT))
    edge = lax.ppermute(normed, AXES, edge_pairs(count))
    chunks, keyval = call(
        project_kernel,
        [SMEM] * 2 + [WHOLE] * 3,
        [jax.ShapeDtypeStruct((HEADS, CHUNK, BLOCK), bf16), jax.ShapeDtypeStruct((HEADS, 2 * HD, BLOCK), bf16)],
        [pltpu.VMEM((2 * BLOCK, width), bf16)],
        20 * 2 * 2 * BLOCK * w_qkv.shape[0] * w_qkv.shape[1],
        6 * 2**20,
        index,
        links,
        normed,
        other,
        w_qkv,
    )
    held = lax.all_to_all(chunks, AXES, 0, 0, axis_index_groups=groups, tiled=True)
    from_edge = call(
        edge_kernel,
        [WHOLE] * 2,
        jax.ShapeDtypeStruct((HEADS, 2 * HD, BLOCK), bf16),
        [],
        40 * 2 * BLOCK * w_qkv.shape[0] * w_qkv.shape[1],
        4 * 2**20,
        edge,
        w_qkv,
    )
    keyval, from_edge = lax.optimization_barrier((keyval, from_edge))
    from_x_lo = lax.ppermute(keyval, AXES, xor_pairs(count, 3))
    from_x_hi = lax.ppermute(keyval, AXES, xor_pairs(count, 5))
    held, from_edge = lax.optimization_barrier((held, from_edge))
    back = call(
        group_kernel,
        [SMEM, WHOLE],
        jax.ShapeDtypeStruct((HEADS, BACK, BLOCK), bf16),
        attend_scratch,
        20 * 64 * 4 * BLOCK * BLOCK * 256,
        3 * 2**20,
        index,
        held,
    )
    mine = lax.all_to_all(back, AXES, 0, 0, axis_index_groups=groups, tiled=True)
    home = call(
        functools.partial(home_kernel, count=count),
        [SMEM] * 2 + [WHOLE] * 4,
        jax.ShapeDtypeStruct((HEADS, HD + 8, BLOCK), f32),
        attend_scratch,
        20 * 32 * 4 * BLOCK * BLOCK * 256,
        4 * 2**20,
        index,
        links,
        chunks,
        from_x_lo,
        from_x_hi,
        from_edge,
    )
    mine, home = lax.optimization_barrier((mine, home))
    theirs = lax.ppermute(mine, AXES, xor_pairs(count, CORE_BIT))
    return call(
        finish_kernel,
        [WHOLE] * 3,
        jax.ShapeDtypeStruct((BLOCK, INNER), f32),
        [],
        10**7,
        2 * 2**20,
        home,
        mine,
        theirs,
    )


def solution(mesh):
    placed = (P(AXES, None), P(), P(), P(), P(AXES))
    return jax.shard_map(
        functools.partial(per_device, count=mesh.size),
        mesh=mesh,
        in_specs=placed,
        out_specs=P(AXES, None),
        check_vma=False,
    )
```

```python
import functools
import math

import jax
import jax.numpy as jnp
from jax import lax
from jax.experimental import pallas as pl
from jax.experimental.pallas import tpu as pltpu
from jax.sharding import PartitionSpec as P

AXES = ("row", "col")
HEADS = 8
HD = 64
BLOCK = 256
INNER = HEADS * HD
WIDE = 3 * HD
SLOTS = 2
KEYS = 4
CHUNK = SLOTS * WIDE + 8
BACK = SLOTS * HD + 8
LOW = -1e30
SCALE = 1.0 / math.sqrt(HD)
LOG2E = math.log2(math.e)
Y_COUNT = 8
CORE_BIT = 4
VMEM_LIMIT = 32 * 1024 * 1024


def fields(index):
    return index & 7, (index >> 3) & 1, (index >> 4) & 1, (index >> 5) & 1, index >> 6


def split_groups(count):
    groups = {}
    for index in range(count):
        y, x_lo, core, x_hi, z = fields(index)
        key = (0, z, x_hi, x_lo) if core == 0 else (1, y, x_hi, x_lo)
        groups.setdefault(key, []).append(index)
    return [groups[key] for key in sorted(groups)]


def xor_pairs(count, bit):
    return [(index, index ^ (1 << bit)) for index in range(count)]


def edge_pairs(count):
    pairs = []
    for index in range(count):
        y = index % Y_COUNT
        if y == Y_COUNT - 1 and index + 1 < count:
            pairs.append((index, index + 1))
        if y == 0 and index > 0:
            pairs.append((index, index - 1))
    return pairs


def normalize(tokens, gain, shift):
    values = tokens.astype(jnp.float32)
    centred = values - jnp.mean(values, axis=-1, keepdims=True)
    row_var = jnp.mean(centred * centred, axis=-1, keepdims=True)
    return (centred * lax.rsqrt(row_var + 1e-05) * gain + shift).astype(jnp.bfloat16)


def key_times(index, links, core):
    y = index & 7
    bits = [(links >> bit) & 1 for bit in range(9)]
    odd = y & 1
    before = jnp.where(y > 0, 1 + odd * bits[0], 0)
    after = jnp.where(y < Y_COUNT - 1, 1 + (1 - odd) * bits[0], 0)
    along_y = (before, after, bits[1], bits[2])
    along_z = (jnp.int32(1), bits[6], bits[7], bits[8])
    return [jnp.where(core == 0, one, two) for one, two in zip(along_y, along_z)]


def key_members(member, core):
    along_y = (jnp.maximum(member - 1, 0), jnp.minimum(member + 1, HEADS - 1), member ^ 2, member ^ 4)
    along_z = (member, member ^ 1, member ^ 2, member ^ 4)
    return [jnp.where(core == 0, one, two) for one, two in zip(along_y, along_z)]


def stack_rows(rows, height, width, kind=jnp.float32):
    line = lax.broadcasted_iota(jnp.int32, (height, width), 0)
    table = jnp.zeros((height, width), kind)
    for entry, row in enumerate(rows):
        table = jnp.where(line == entry, row, table)
    return table


def norm_kernel(index_ref, links_ref, tokens_ref, affine_ref, out_ref):
    index = index_ref[0]
    times = key_times(index, links_ref[0], 1 - ((index >> CORE_BIT) & 1))
    out_ref[BLOCK:, :] = stack_rows(times, 16, out_ref.shape[1], jnp.int32).astype(jnp.float32).astype(jnp.bfloat16)
    out_ref[:BLOCK, :] = normalize(tokens_ref[...], affine_ref[0:1, :], affine_ref[1:2, :])


def project(normed_ref, w_ref, kinds, store, starts=(0, 4 * HD)):
    tile = 4 * HD
    for kind in kinds:
        for start in starts:
            columns = w_ref[:, kind * INNER + start : kind * INNER + start + tile]
            product = jnp.dot(normed_ref[...], columns, preferred_element_type=jnp.float32)
            turned = product.T.astype(jnp.bfloat16)
            for local in range(4):
                store(kind, start // HD + local, turned[local * HD : (local + 1) * HD])


def project_kernel(index_ref, links_ref, own_ref, other_ref, w_ref, chunk_hbm, keyval_ref, normed_ref, chunk_ref, sems):
    index = index_ref[0]
    times = key_times(index, links_ref[0], (index >> CORE_BIT) & 1)
    table = stack_rows(times, 8, BLOCK, jnp.int32).astype(jnp.float32)
    sent = other_ref[BLOCK:, :BLOCK].astype(jnp.float32)
    line = lax.broadcasted_iota(jnp.int32, (8, BLOCK), 0)
    for entry in range(KEYS):
        table = jnp.where(line == KEYS + entry, sent[entry : entry + 1], table)
    for head in range(HEADS):
        chunk_ref[head, SLOTS * WIDE :, :] = table.astype(jnp.bfloat16)
    normed_ref[:BLOCK] = own_ref[:BLOCK]
    normed_ref[BLOCK:] = other_ref[:BLOCK]

    def store(kind, head, rows):
        for slot in range(SLOTS):
            start = slot * WIDE + kind * HD
            chunk_ref[head, start : start + HD, :] = rows[:, slot * BLOCK : (slot + 1) * BLOCK]
        if kind > 0:
            keyval_ref[head, (kind - 1) * HD : kind * HD, :] = rows[:, :BLOCK]

    half = HEADS // 2
    sends = []
    for at in range(2):
        project(normed_ref, w_ref, (0, 1, 2), store, (at * half * HD,))
        heads = pl.ds(at * half, half)
        sends.append(pltpu.make_async_copy(chunk_ref.at[heads], chunk_hbm.at[heads], sems.at[at]))
        sends[-1].start()
    for send in sends:
        send.wait()


def edge_kernel(normed_ref, w_ref, keyval_ref):
    def store(kind, head, rows):
        keyval_ref[head, (kind - 1) * HD : kind * HD, :] = rows

    project(normed_ref.at[pl.ds(0, BLOCK)], w_ref, (1, 2), store)


def attend_all(items, score_ref, weight_ref, key_dim=0):
    for at, (query, key, _) in enumerate(items):
        score_ref[at] = lax.dot_general(
            key(), query(), (((key_dim,), (0,)), ((), ())), preferred_element_type=jnp.float32
        )
    stats = []
    for at in range(len(items)):
        scores = score_ref[at]
        peak = jnp.max(scores, axis=0, keepdims=True)
        weights = jnp.exp2((scores - peak) * (SCALE * LOG2E))
        stats.append((peak * SCALE, jnp.sum(weights, axis=0, keepdims=True)))
        weight_ref[at] = weights.astype(jnp.bfloat16)
    return [
        (jnp.dot(value(), weight_ref[at], preferred_element_type=jnp.float32),) + stats[at]
        for at, (_, _, value) in enumerate(items)
    ]


def merge(items):
    maxima = [jnp.where(times > 0, peak, LOW) for _, peak, _, times in items]
    top = functools.reduce(jnp.maximum, maxima)
    accum = total = None
    for (value, _, row_sum, times), peak in zip(items, maxima):
        factor = times * jnp.exp2((peak - top) * LOG2E)
        value, row_sum = factor * value.astype(jnp.bfloat16).astype(jnp.float32), factor * row_sum
        accum = value if accum is None else accum + value
        total = row_sum if total is None else total + row_sum
    return accum, top, total


def thirds(value):
    high = value.astype(jnp.bfloat16).astype(jnp.float32)
    rest = value - high
    middle = rest.astype(jnp.bfloat16).astype(jnp.float32)
    return [high, middle, rest - middle]


def group_kernel(index_ref, held_ref, back_hbm, score_ref, weight_ref, key_ref, back_ref, sems):
    core = (index_ref[0] >> CORE_BIT) & 1
    for source in range(HEADS):
        for slot in range(SLOTS):
            start = slot * WIDE + HD
            key_ref[source, slot] = held_ref[source, start : start + HD, :].T

    def step(member, carry):
        table = held_ref[member, SLOTS * WIDE :, :].astype(jnp.float32)
        sources = key_members(member, core)
        load = lambda source, start: lambda: held_ref[source, start : start + HD, :]
        turned = lambda source, slot: lambda: key_ref[source, slot]
        items = [
            (load(member, slot * WIDE), turned(source, slot), load(source, slot * WIDE + 2 * HD))
            for slot in range(SLOTS)
            for source in sources
        ]
        results = attend_all(items, score_ref, weight_ref, 1)
        stats = []
        for slot in range(SLOTS):
            at = slot * KEYS
            accum, top, total = merge(
                [results[at + entry] + (table[at + entry : at + entry + 1],) for entry in range(KEYS)]
            )
            back_ref[member, slot * HD : (slot + 1) * HD, :] = (accum / total).astype(jnp.bfloat16)
            stats.extend(thirds(top + jnp.log(total)))
        back_ref[member, SLOTS * HD :, :] = stack_rows(stats, 8, BLOCK).astype(jnp.bfloat16)
        pltpu.make_async_copy(back_ref.at[member], back_hbm.at[member], sems.at[member]).start()
        return carry

    lax.fori_loop(0, HEADS, step, 0)
    for member in range(HEADS):
        pltpu.make_async_copy(back_ref.at[member], back_hbm.at[member], sems.at[member]).wait()


def home_kernel(index_ref, links_ref, chunk_ref, x_lo_ref, x_hi_ref, edge_ref, out_ref, score_ref, weight_ref, count):
    index = index_ref[0]
    y = index & 7
    outer = ((y == 0) & (index > 0)) | ((y == Y_COUNT - 1) & (index < count - 1))
    times = [(links_ref[0] >> bit) & 1 for bit in (4, 3, 5)] + [jnp.where(outer, 1, 0)]
    rows = [jnp.full((1, BLOCK), number, jnp.int32).astype(jnp.float32) for number in times]

    def step(pair, carry):
        items = []
        load = lambda ref, head, start: lambda: ref[head, start : start + HD, :]
        for head in (2 * pair, 2 * pair + 1):
            query = load(chunk_ref, head, 0)
            items.append((query, load(chunk_ref, head, WIDE + HD), load(chunk_ref, head, WIDE + 2 * HD)))
            for ref in (x_lo_ref, x_hi_ref, edge_ref):
                items.append((query, load(ref, head, 0), load(ref, head, HD)))
        results = attend_all(items, score_ref, weight_ref)
        for local in range(2):
            accum, top, total = merge([results[local * KEYS + entry] + (rows[entry],) for entry in range(KEYS)])
            head = 2 * pair + local
            out_ref[head, :HD, :] = accum
            out_ref[head, HD:, :] = stack_rows([top, total], 8, BLOCK)
        return carry

    lax.fori_loop(0, HEADS // 2, step, 0)


def finish_kernel(home_ref, own_ref, other_ref, out_ref):
    for pair in range(HEADS // 2):
        turned = []
        for head in (2 * pair, 2 * pair + 1):
            home_top = home_ref[head, HD : HD + 1, :]
            parts = [(home_ref[head, :HD, :], home_top, home_ref[head, HD + 1 : HD + 2, :])]
            for ref, slot in ((own_ref, 0), (other_ref, 1)):
                value = ref[head, slot * HD : (slot + 1) * HD, :].astype(jnp.float32)
                stats = ref[head, SLOTS * HD :, :].astype(jnp.float32)
                at = 3 * slot
                parts.append((value, stats[at : at + 1] + stats[at + 1 : at + 2] + stats[at + 2 : at + 3], 1.0))
            top = functools.reduce(jnp.maximum, [peak for _, peak, _ in parts])
            factors = [jnp.exp2((peak - top) * LOG2E) for _, peak, _ in parts]
            accum = sum(factor * value for factor, (value, _, _) in zip(factors, parts))
            total = sum(factor * row_sum for factor, (_, _, row_sum) in zip(factors, parts))
            turned.append(accum / total)
        out_ref[:, pair * 2 * HD : (pair + 1) * 2 * HD] = jnp.concatenate(turned, axis=0).T


SMEM = pl.BlockSpec(memory_space=pltpu.SMEM)
WHOLE = pl.BlockSpec(memory_space=pltpu.VMEM)
HBM = pl.BlockSpec(memory_space=pltpu.HBM)


def call(kernel, specs, shapes, scratch, flops, moved, *operands, limit=VMEM_LIMIT, outs=None):
    return pl.pallas_call(
        kernel,
        in_specs=specs,
        out_specs=outs or ([WHOLE] * len(shapes) if isinstance(shapes, list) else WHOLE),
        out_shape=shapes,
        scratch_shapes=scratch,
        compiler_params=pltpu.CompilerParams(vmem_limit_bytes=limit),
        cost_estimate=pl.CostEstimate(flops=flops, bytes_accessed=moved, transcendentals=0),
    )(*operands)


def per_device(tokens, norm_gain, norm_shift, w_qkv, links, count):
    groups = split_groups(count)
    width = w_qkv.shape[0]
    bf16, f32 = jnp.bfloat16, jnp.float32
    index = (lax.axis_index("row") * lax.axis_size("col") + lax.axis_index("col")).astype(jnp.int32)[None]
    attend_scratch = [pltpu.VMEM((2 * KEYS, BLOCK, BLOCK), f32), pltpu.VMEM((2 * KEYS, BLOCK, BLOCK), bf16)]
    normed = call(
        norm_kernel,
        [SMEM] * 2 + [WHOLE] * 2,
        jax.ShapeDtypeStruct((BLOCK + 16, width), bf16),
        [],
        13 * 10**9,
        2**20,
        index,
        links,
        tokens,
        jnp.stack([norm_gain, norm_shift]),
    )
    other = lax.ppermute(normed, AXES, xor_pairs(count, CORE_BIT))
    edge = lax.ppermute(normed, AXES, edge_pairs(count))
    chunks, keyval = call(
        project_kernel,
        [SMEM] * 2 + [WHOLE] * 3,
        [jax.ShapeDtypeStruct((HEADS, CHUNK, BLOCK), bf16), jax.ShapeDtypeStruct((HEADS, 2 * HD, BLOCK), bf16)],
        [
            pltpu.VMEM((2 * BLOCK, width), bf16),
            pltpu.VMEM((HEADS, CHUNK, BLOCK), bf16),
            pltpu.SemaphoreType.DMA((2,)),
        ],
        20 * 2 * 2 * BLOCK * w_qkv.shape[0] * w_qkv.shape[1],
        6 * 2**20,
        index,
        links,
        normed,
        other,
        w_qkv,
        outs=[HBM, WHOLE],
    )
    held = lax.all_to_all(chunks, AXES, 0, 0, axis_index_groups=groups, tiled=True)
    from_edge = call(
        edge_kernel,
        [WHOLE] * 2,
        jax.ShapeDtypeStruct((HEADS, 2 * HD, BLOCK), bf16),
        [],
        40 * 2 * BLOCK * w_qkv.shape[0] * w_qkv.shape[1],
        4 * 2**20,
        edge,
        w_qkv,
    )
    keyval, from_edge = lax.optimization_barrier((keyval, from_edge))
    from_x_lo = lax.ppermute(keyval, AXES, xor_pairs(count, 3))
    from_x_hi = lax.ppermute(keyval, AXES, xor_pairs(count, 5))
    held, from_edge = lax.optimization_barrier((held, from_edge))
    back = call(
        group_kernel,
        [SMEM, WHOLE],
        jax.ShapeDtypeStruct((HEADS, BACK, BLOCK), bf16),
        attend_scratch
        + [pltpu.VMEM((HEADS, SLOTS, BLOCK, HD), bf16), pltpu.VMEM((HEADS, BACK, BLOCK), bf16), pltpu.SemaphoreType.DMA((HEADS,))],
        20 * 64 * 4 * BLOCK * BLOCK * 256,
        3 * 2**20,
        index,
        held,
        outs=HBM,
    )
    mine = lax.all_to_all(back, AXES, 0, 0, axis_index_groups=groups, tiled=True)
    home = call(
        functools.partial(home_kernel, count=count),
        [SMEM] * 2 + [WHOLE] * 4,
        jax.ShapeDtypeStruct((HEADS, HD + 8, BLOCK), f32),
        attend_scratch,
        20 * 32 * 4 * BLOCK * BLOCK * 256,
        4 * 2**20,
        index,
        links,
        chunks,
        from_x_lo,
        from_x_hi,
        from_edge,
    )
    mine, home = lax.optimization_barrier((mine, home))
    theirs = lax.ppermute(mine, AXES, xor_pairs(count, CORE_BIT))
    return call(
        finish_kernel,
        [WHOLE] * 3,
        jax.ShapeDtypeStruct((BLOCK, INNER), f32),
        [],
        10**7,
        2 * 2**20,
        home,
        mine,
        theirs,
    )


def solution(mesh):
    placed = (P(AXES, None), P(), P(), P(), P(AXES))
    return jax.shard_map(
        functools.partial(per_device, count=mesh.size),
        mesh=mesh,
        in_specs=placed,
        out_specs=P(AXES, None),
        check_vma=False,
    )
```

```python
import functools
import math

import jax
import jax.numpy as jnp
from jax import lax
from jax.experimental import pallas as pl
from jax.experimental.pallas import tpu as pltpu
from jax.sharding import PartitionSpec as P

AXES = ("row", "col")
HEADS = 8
HD = 64
BLOCK = 256
INNER = HEADS * HD
WIDE = 3 * HD
SLOTS = 2
KEYS = 4
CHUNK = SLOTS * WIDE + 8
BACK = SLOTS * HD + 8
LOW = -1e30
SCALE = 1.0 / math.sqrt(HD)
LOG2E = math.log2(math.e)
Y_COUNT = 8
STRIDE = 3
CORE_BIT = 4
VMEM_LIMIT = 32 * 1024 * 1024


def fields(index):
    return index & 7, (index >> 3) & 1, (index >> 4) & 1, (index >> 5) & 1, index >> 6


def split_groups(count):
    groups = {}
    for index in range(count):
        y, x_lo, core, x_hi, z = fields(index)
        key = (0, z, x_hi, x_lo) if core == 0 else (1, y, x_hi, x_lo)
        groups.setdefault(key, []).append(index)
    return [[groups[key][at * STRIDE % HEADS] for at in range(HEADS)] for key in sorted(groups)]


def xor_pairs(count, bit):
    return [(index, index ^ (1 << bit)) for index in range(count)]


def edge_pairs(count):
    pairs = []
    for index in range(count):
        y = index % Y_COUNT
        if y == Y_COUNT - 1 and index + 1 < count:
            pairs.append((index, index + 1))
        if y == 0 and index > 0:
            pairs.append((index, index - 1))
    return pairs


def normalize(tokens, gain, shift):
    values = tokens.astype(jnp.float32)
    centred = values - jnp.mean(values, axis=-1, keepdims=True)
    row_var = jnp.mean(centred * centred, axis=-1, keepdims=True)
    return (centred * lax.rsqrt(row_var + 1e-05) * gain + shift).astype(jnp.bfloat16)


def key_times(index, links, core):
    y = index & 7
    bits = [(links >> bit) & 1 for bit in range(9)]
    odd = y & 1
    before = jnp.where(y > 0, 1 + odd * bits[0], 0)
    after = jnp.where(y < Y_COUNT - 1, 1 + (1 - odd) * bits[0], 0)
    along_y = (before, after, bits[1], bits[2])
    along_z = (jnp.int32(1), bits[6], bits[7], bits[8])
    return [jnp.where(core == 0, one, two) for one, two in zip(along_y, along_z)]


def key_members(member, core):
    place = (member * STRIDE) & (HEADS - 1)
    along_y = (jnp.maximum(place - 1, 0), jnp.minimum(place + 1, HEADS - 1), place ^ 2, place ^ 4)
    along_z = (place, place ^ 1, place ^ 2, place ^ 4)
    places = [jnp.where(core == 0, one, two) for one, two in zip(along_y, along_z)]
    return [(at * STRIDE) & (HEADS - 1) for at in places]


def stack_rows(rows, height, width, kind=jnp.float32):
    line = lax.broadcasted_iota(jnp.int32, (height, width), 0)
    table = jnp.zeros((height, width), kind)
    for entry, row in enumerate(rows):
        table = jnp.where(line == entry, row, table)
    return table


def norm_kernel(index_ref, links_ref, tokens_ref, affine_ref, out_ref):
    index = index_ref[0]
    times = key_times(index, links_ref[0], 1 - ((index >> CORE_BIT) & 1))
    out_ref[BLOCK:, :] = stack_rows(times, 16, out_ref.shape[1], jnp.int32).astype(jnp.float32).astype(jnp.bfloat16)
    out_ref[:BLOCK, :] = normalize(tokens_ref[...], affine_ref[0:1, :], affine_ref[1:2, :])


def project(normed_ref, w_ref, kinds, store, starts=(0, 4 * HD)):
    tile = 4 * HD
    for kind in kinds:
        for start in starts:
            columns = w_ref[:, kind * INNER + start : kind * INNER + start + tile]
            product = jnp.dot(normed_ref[...], columns, preferred_element_type=jnp.float32)
            turned = product.T.astype(jnp.bfloat16)
            for local in range(4):
                store(kind, start // HD + local, turned[local * HD : (local + 1) * HD])


def project_kernel(index_ref, links_ref, own_ref, other_ref, w_ref, chunk_hbm, keyval_ref, normed_ref, chunk_ref, sems):
    index = index_ref[0]
    times = key_times(index, links_ref[0], (index >> CORE_BIT) & 1)
    table = stack_rows(times, 8, BLOCK, jnp.int32).astype(jnp.float32)
    sent = other_ref[BLOCK:, :BLOCK].astype(jnp.float32)
    line = lax.broadcasted_iota(jnp.int32, (8, BLOCK), 0)
    for entry in range(KEYS):
        table = jnp.where(line == KEYS + entry, sent[entry : entry + 1], table)
    for head in range(HEADS):
        chunk_ref[head, SLOTS * WIDE :, :] = table.astype(jnp.bfloat16)
    normed_ref[:BLOCK] = own_ref[:BLOCK]
    normed_ref[BLOCK:] = other_ref[:BLOCK]

    def store(kind, head, rows):
        for slot in range(SLOTS):
            start = slot * WIDE + kind * HD
            chunk_ref[head, start : start + HD, :] = rows[:, slot * BLOCK : (slot + 1) * BLOCK]
        if kind > 0:
            keyval_ref[head, (kind - 1) * HD : kind * HD, :] = rows[:, :BLOCK]

    half = HEADS // 2
    sends = []
    for at in range(2):
        project(normed_ref, w_ref, (0, 1, 2), store, (at * half * HD,))
        heads = pl.ds(at * half, half)
        sends.append(pltpu.make_async_copy(chunk_ref.at[heads], chunk_hbm.at[heads], sems.at[at]))
        sends[-1].start()
    for send in sends:
        send.wait()


def edge_kernel(normed_ref, w_ref, keyval_ref):
    def store(kind, head, rows):
        keyval_ref[head, (kind - 1) * HD : kind * HD, :] = rows

    project(normed_ref.at[pl.ds(0, BLOCK)], w_ref, (1, 2), store)


def attend_all(items, score_ref, weight_ref, key_dim=0):
    for at, (query, key, _) in enumerate(items):
        score_ref[at] = lax.dot_general(
            key(), query(), (((key_dim,), (0,)), ((), ())), preferred_element_type=jnp.float32
        )
    stats = []
    for at in range(len(items)):
        scores = score_ref[at]
        peak = jnp.max(scores, axis=0, keepdims=True)
        weights = jnp.exp2((scores - peak) * (SCALE * LOG2E))
        stats.append((peak * SCALE, jnp.sum(weights, axis=0, keepdims=True)))
        weight_ref[at] = weights.astype(jnp.bfloat16)
    return [
        (jnp.dot(value(), weight_ref[at], preferred_element_type=jnp.float32),) + stats[at]
        for at, (_, _, value) in enumerate(items)
    ]


def merge(items):
    maxima = [jnp.where(times > 0, peak, LOW) for _, peak, _, times in items]
    top = functools.reduce(jnp.maximum, maxima)
    accum = total = None
    for (value, _, row_sum, times), peak in zip(items, maxima):
        factor = times * jnp.exp2((peak - top) * LOG2E)
        value, row_sum = factor * value.astype(jnp.bfloat16).astype(jnp.float32), factor * row_sum
        accum = value if accum is None else accum + value
        total = row_sum if total is None else total + row_sum
    return accum, top, total


def thirds(value):
    high = value.astype(jnp.bfloat16).astype(jnp.float32)
    rest = value - high
    middle = rest.astype(jnp.bfloat16).astype(jnp.float32)
    return [high, middle, rest - middle]


def group_kernel(index_ref, held_ref, back_hbm, score_ref, weight_ref, key_ref, back_ref, sems):
    core = (index_ref[0] >> CORE_BIT) & 1
    for source in range(HEADS):
        for slot in range(SLOTS):
            start = slot * WIDE + HD
            key_ref[source, slot] = held_ref[source, start : start + HD, :].T

    def step(member, carry):
        table = held_ref[member, SLOTS * WIDE :, :].astype(jnp.float32)
        sources = key_members(member, core)
        load = lambda source, start: lambda: held_ref[source, start : start + HD, :]
        turned = lambda source, slot: lambda: key_ref[source, slot]
        items = [
            (load(member, slot * WIDE), turned(source, slot), load(source, slot * WIDE + 2 * HD))
            for slot in range(SLOTS)
            for source in sources
        ]
        results = attend_all(items, score_ref, weight_ref, 1)
        stats = []
        for slot in range(SLOTS):
            at = slot * KEYS
            accum, top, total = merge(
                [results[at + entry] + (table[at + entry : at + entry + 1],) for entry in range(KEYS)]
            )
            back_ref[member, slot * HD : (slot + 1) * HD, :] = (accum / total).astype(jnp.bfloat16)
            stats.extend(thirds(top + jnp.log(total)))
        back_ref[member, SLOTS * HD :, :] = stack_rows(stats, 8, BLOCK).astype(jnp.bfloat16)
        pltpu.make_async_copy(back_ref.at[member], back_hbm.at[member], sems.at[member]).start()
        return carry

    lax.fori_loop(0, HEADS, step, 0)
    for member in range(HEADS):
        pltpu.make_async_copy(back_ref.at[member], back_hbm.at[member], sems.at[member]).wait()


def home_kernel(index_ref, links_ref, chunk_ref, x_lo_ref, x_hi_ref, edge_ref, out_ref, score_ref, weight_ref, count):
    index = index_ref[0]
    y = index & 7
    outer = ((y == 0) & (index > 0)) | ((y == Y_COUNT - 1) & (index < count - 1))
    times = [(links_ref[0] >> bit) & 1 for bit in (4, 3, 5)] + [jnp.where(outer, 1, 0)]
    rows = [jnp.full((1, BLOCK), number, jnp.int32).astype(jnp.float32) for number in times]

    def step(pair, carry):
        items = []
        load = lambda ref, head, start: lambda: ref[head, start : start + HD, :]
        for head in (2 * pair, 2 * pair + 1):
            query = load(chunk_ref, head, 0)
            items.append((query, load(chunk_ref, head, WIDE + HD), load(chunk_ref, head, WIDE + 2 * HD)))
            for ref in (x_lo_ref, x_hi_ref, edge_ref):
                items.append((query, load(ref, head, 0), load(ref, head, HD)))
        results = attend_all(items, score_ref, weight_ref)
        for local in range(2):
            accum, top, total = merge([results[local * KEYS + entry] + (rows[entry],) for entry in range(KEYS)])
            head = 2 * pair + local
            out_ref[head, :HD, :] = accum
            out_ref[head, HD:, :] = stack_rows([top, total], 8, BLOCK)
        return carry

    lax.fori_loop(0, HEADS // 2, step, 0)


def finish_kernel(home_ref, own_ref, other_ref, out_ref):
    for pair in range(HEADS // 2):
        turned = []
        for head in (2 * pair, 2 * pair + 1):
            home_top = home_ref[head, HD : HD + 1, :]
            parts = [(home_ref[head, :HD, :], home_top, home_ref[head, HD + 1 : HD + 2, :])]
            for ref, slot in ((own_ref, 0), (other_ref, 1)):
                value = ref[head, slot * HD : (slot + 1) * HD, :].astype(jnp.float32)
                stats = ref[head, SLOTS * HD :, :].astype(jnp.float32)
                at = 3 * slot
                parts.append((value, stats[at : at + 1] + stats[at + 1 : at + 2] + stats[at + 2 : at + 3], 1.0))
            top = functools.reduce(jnp.maximum, [peak for _, peak, _ in parts])
            factors = [jnp.exp2((peak - top) * LOG2E) for _, peak, _ in parts]
            accum = sum(factor * value for factor, (value, _, _) in zip(factors, parts))
            total = sum(factor * row_sum for factor, (_, _, row_sum) in zip(factors, parts))
            turned.append(accum / total)
        out_ref[:, pair * 2 * HD : (pair + 1) * 2 * HD] = jnp.concatenate(turned, axis=0).T


SMEM = pl.BlockSpec(memory_space=pltpu.SMEM)
WHOLE = pl.BlockSpec(memory_space=pltpu.VMEM)
HBM = pl.BlockSpec(memory_space=pltpu.HBM)


def call(kernel, specs, shapes, scratch, flops, moved, *operands, limit=VMEM_LIMIT, outs=None):
    return pl.pallas_call(
        kernel,
        in_specs=specs,
        out_specs=outs or ([WHOLE] * len(shapes) if isinstance(shapes, list) else WHOLE),
        out_shape=shapes,
        scratch_shapes=scratch,
        compiler_params=pltpu.CompilerParams(vmem_limit_bytes=limit),
        cost_estimate=pl.CostEstimate(flops=flops, bytes_accessed=moved, transcendentals=0),
    )(*operands)


def per_device(tokens, norm_gain, norm_shift, w_qkv, links, count):
    groups = split_groups(count)
    width = w_qkv.shape[0]
    bf16, f32 = jnp.bfloat16, jnp.float32
    index = (lax.axis_index("row") * lax.axis_size("col") + lax.axis_index("col")).astype(jnp.int32)[None]
    attend_scratch = [pltpu.VMEM((2 * KEYS, BLOCK, BLOCK), f32), pltpu.VMEM((2 * KEYS, BLOCK, BLOCK), bf16)]
    normed = call(
        norm_kernel,
        [SMEM] * 2 + [WHOLE] * 2,
        jax.ShapeDtypeStruct((BLOCK + 16, width), bf16),
        [],
        13 * 10**9,
        2**20,
        index,
        links,
        tokens,
        jnp.stack([norm_gain, norm_shift]),
    )
    other = lax.ppermute(normed, AXES, xor_pairs(count, CORE_BIT))
    edge = lax.ppermute(normed, AXES, edge_pairs(count))
    chunks, keyval = call(
        project_kernel,
        [SMEM] * 2 + [WHOLE] * 3,
        [jax.ShapeDtypeStruct((HEADS, CHUNK, BLOCK), bf16), jax.ShapeDtypeStruct((HEADS, 2 * HD, BLOCK), bf16)],
        [
            pltpu.VMEM((2 * BLOCK, width), bf16),
            pltpu.VMEM((HEADS, CHUNK, BLOCK), bf16),
            pltpu.SemaphoreType.DMA((2,)),
        ],
        20 * 2 * 2 * BLOCK * w_qkv.shape[0] * w_qkv.shape[1],
        6 * 2**20,
        index,
        links,
        normed,
        other,
        w_qkv,
        outs=[HBM, WHOLE],
    )
    held = lax.all_to_all(chunks, AXES, 0, 0, axis_index_groups=groups, tiled=True)
    from_edge = call(
        edge_kernel,
        [WHOLE] * 2,
        jax.ShapeDtypeStruct((HEADS, 2 * HD, BLOCK), bf16),
        [],
        30 * 2 * BLOCK * w_qkv.shape[0] * w_qkv.shape[1],
        4 * 2**20,
        edge,
        w_qkv,
    )
    from_x_lo = lax.ppermute(keyval, AXES, xor_pairs(count, 3))
    from_x_hi = lax.ppermute(keyval, AXES, xor_pairs(count, 5))
    held, from_edge = lax.optimization_barrier((held, from_edge))
    back = call(
        group_kernel,
        [SMEM, WHOLE],
        jax.ShapeDtypeStruct((HEADS, BACK, BLOCK), bf16),
        attend_scratch
        + [pltpu.VMEM((HEADS, SLOTS, BLOCK, HD), bf16), pltpu.VMEM((HEADS, BACK, BLOCK), bf16), pltpu.SemaphoreType.DMA((HEADS,))],
        20 * 64 * 4 * BLOCK * BLOCK * 256,
        3 * 2**20,
        index,
        held,
        outs=HBM,
    )
    mine = lax.all_to_all(back, AXES, 0, 0, axis_index_groups=groups, tiled=True)
    home = call(
        functools.partial(home_kernel, count=count),
        [SMEM] * 2 + [WHOLE] * 4,
        jax.ShapeDtypeStruct((HEADS, HD + 8, BLOCK), f32),
        attend_scratch,
        20 * 32 * 4 * BLOCK * BLOCK * 256,
        4 * 2**20,
        index,
        links,
        chunks,
        from_x_lo,
        from_x_hi,
        from_edge,
    )
    mine, home = lax.optimization_barrier((mine, home))
    theirs = lax.ppermute(mine, AXES, xor_pairs(count, CORE_BIT))
    return call(
        finish_kernel,
        [WHOLE] * 3,
        jax.ShapeDtypeStruct((BLOCK, INNER), f32),
        [],
        10**7,
        2 * 2**20,
        home,
        mine,
        theirs,
    )


def solution(mesh):
    placed = (P(AXES, None), P(), P(), P(), P(AXES))
    return jax.shard_map(
        functools.partial(per_device, count=mesh.size),
        mesh=mesh,
        in_specs=placed,
        out_specs=P(AXES, None),
        check_vma=False,
    )
```

```python
import functools
import math

import jax
import jax.numpy as jnp
from jax import lax
from jax.experimental import pallas as pl
from jax.experimental.pallas import tpu as pltpu
from jax.sharding import PartitionSpec as P

AXES = ("row", "col")
HEADS = 8
HD = 64
BLOCK = 256
INNER = HEADS * HD
WIDE = 3 * HD
SLOTS = 2
KEYS = 4
CHUNK = SLOTS * WIDE + 8
BACK = SLOTS * HD + 8
LOW = -1e30
SCALE = 1.0 / math.sqrt(HD)
LOG2E = math.log2(math.e)
Y_COUNT = 8
STRIDE = 3
CORE_BIT = 4
VMEM_LIMIT = 32 * 1024 * 1024


def fields(index):
    return index & 7, (index >> 3) & 1, (index >> 4) & 1, (index >> 5) & 1, index >> 6


def split_groups(count):
    groups = {}
    for index in range(count):
        y, x_lo, core, x_hi, z = fields(index)
        key = (0, z, x_hi, x_lo) if core == 0 else (1, y, x_hi, x_lo)
        groups.setdefault(key, []).append(index)
    return [[groups[key][at * STRIDE % HEADS] for at in range(HEADS)] for key in sorted(groups)]


def xor_pairs(count, bit):
    return [(index, index ^ (1 << bit)) for index in range(count)]


def edge_pairs(count):
    pairs = []
    for index in range(count):
        y = index % Y_COUNT
        if y == Y_COUNT - 1 and index + 1 < count:
            pairs.append((index, index + 1))
        if y == 0 and index > 0:
            pairs.append((index, index - 1))
    return pairs


def normalize(tokens, gain, shift):
    values = tokens.astype(jnp.float32)
    centred = values - jnp.mean(values, axis=-1, keepdims=True)
    row_var = jnp.mean(centred * centred, axis=-1, keepdims=True)
    return (centred * lax.rsqrt(row_var + 1e-05) * gain + shift).astype(jnp.bfloat16)


def key_times(index, links, core):
    y = index & 7
    bits = [(links >> bit) & 1 for bit in range(9)]
    odd = y & 1
    before = jnp.where(y > 0, 1 + odd * bits[0], 0)
    after = jnp.where(y < Y_COUNT - 1, 1 + (1 - odd) * bits[0], 0)
    along_y = (before, after, bits[1], bits[2])
    along_z = (jnp.int32(1), bits[6], bits[7], bits[8])
    return [jnp.where(core == 0, one, two) for one, two in zip(along_y, along_z)]


def key_members(member, core):
    place = (member * STRIDE) & (HEADS - 1)
    along_y = (jnp.maximum(place - 1, 0), jnp.minimum(place + 1, HEADS - 1), place ^ 2, place ^ 4)
    along_z = (place, place ^ 1, place ^ 2, place ^ 4)
    places = [jnp.where(core == 0, one, two) for one, two in zip(along_y, along_z)]
    return [(at * STRIDE) & (HEADS - 1) for at in places]


def stack_rows(rows, height, width, kind=jnp.float32):
    line = lax.broadcasted_iota(jnp.int32, (height, width), 0)
    table = jnp.zeros((height, width), kind)
    for entry, row in enumerate(rows):
        table = jnp.where(line == entry, row, table)
    return table


def norm_kernel(index_ref, links_ref, tokens_ref, affine_ref, out_ref):
    index = index_ref[0]
    times = key_times(index, links_ref[0], 1 - ((index >> CORE_BIT) & 1))
    out_ref[BLOCK:, :] = stack_rows(times, 16, out_ref.shape[1], jnp.int32).astype(jnp.float32).astype(jnp.bfloat16)
    out_ref[:BLOCK, :] = normalize(tokens_ref[...], affine_ref[0:1, :], affine_ref[1:2, :])


def project(normed_ref, w_ref, kinds, store, starts=(0, 4 * HD)):
    tile = 4 * HD
    for kind in kinds:
        for start in starts:
            columns = w_ref[:, kind * INNER + start : kind * INNER + start + tile]
            product = jnp.dot(normed_ref[...], columns, preferred_element_type=jnp.float32)
            turned = product.T.astype(jnp.bfloat16)
            for local in range(4):
                store(kind, start // HD + local, turned[local * HD : (local + 1) * HD])


def project_kernel(index_ref, links_ref, own_ref, other_ref, w_ref, chunk_hbm, keyval_ref, normed_ref, chunk_ref, sems):
    index = index_ref[0]
    times = key_times(index, links_ref[0], (index >> CORE_BIT) & 1)
    table = stack_rows(times, 8, BLOCK, jnp.int32).astype(jnp.float32)
    sent = other_ref[BLOCK:, :BLOCK].astype(jnp.float32)
    line = lax.broadcasted_iota(jnp.int32, (8, BLOCK), 0)
    for entry in range(KEYS):
        table = jnp.where(line == KEYS + entry, sent[entry : entry + 1], table)
    for head in range(HEADS):
        chunk_ref[head, SLOTS * WIDE :, :] = table.astype(jnp.bfloat16)
    normed_ref[:BLOCK] = own_ref[:BLOCK]
    normed_ref[BLOCK:] = other_ref[:BLOCK]

    def store(kind, head, rows):
        for slot in range(SLOTS):
            start = slot * WIDE + kind * HD
            chunk_ref[head, start : start + HD, :] = rows[:, slot * BLOCK : (slot + 1) * BLOCK]
        if kind > 0:
            keyval_ref[head, (kind - 1) * HD : kind * HD, :] = rows[:, :BLOCK]

    half = HEADS // 2
    sends = []
    for at in range(2):
        project(normed_ref, w_ref, (0, 1, 2), store, (at * half * HD,))
        heads = pl.ds(at * half, half)
        sends.append(pltpu.make_async_copy(chunk_ref.at[heads], chunk_hbm.at[heads], sems.at[at]))
        sends[-1].start()
    for send in sends:
        send.wait()


def edge_kernel(normed_ref, w_ref, keyval_ref):
    def store(kind, head, rows):
        keyval_ref[head, (kind - 1) * HD : kind * HD, :] = rows

    project(normed_ref.at[pl.ds(0, BLOCK)], w_ref, (1, 2), store)


def attend_all(items, score_ref, weight_ref, key_dim=0):
    for at, (query, key, _) in enumerate(items):
        score_ref[at] = lax.dot_general(
            key(), query(), (((key_dim,), (0,)), ((), ())), preferred_element_type=jnp.float32
        )
    stats = []
    for at in range(len(items)):
        scores = score_ref[at]
        peak = jnp.max(scores, axis=0, keepdims=True)
        weights = jnp.exp2((scores - peak) * (SCALE * LOG2E))
        stats.append((peak * SCALE, jnp.sum(weights, axis=0, keepdims=True)))
        weight_ref[at] = weights.astype(jnp.bfloat16)
    return [
        (jnp.dot(value(), weight_ref[at], preferred_element_type=jnp.float32),) + stats[at]
        for at, (_, _, value) in enumerate(items)
    ]


def merge(items):
    maxima = [jnp.where(times > 0, peak, LOW) for _, peak, _, times in items]
    top = functools.reduce(jnp.maximum, maxima)
    accum = total = None
    for (value, _, row_sum, times), peak in zip(items, maxima):
        factor = times * jnp.exp2((peak - top) * LOG2E)
        value, row_sum = factor * value.astype(jnp.bfloat16).astype(jnp.float32), factor * row_sum
        accum = value if accum is None else accum + value
        total = row_sum if total is None else total + row_sum
    return accum, top, total


def thirds(value):
    high = value.astype(jnp.bfloat16).astype(jnp.float32)
    rest = value - high
    middle = rest.astype(jnp.bfloat16).astype(jnp.float32)
    return [high, middle, rest - middle]


def group_kernel(index_ref, held_ref, back_hbm, score_ref, weight_ref, key_ref, back_ref, sems):
    core = (index_ref[0] >> CORE_BIT) & 1
    for source in range(HEADS):
        for slot in range(SLOTS):
            start = slot * WIDE + HD
            key_ref[source, slot] = held_ref[source, start : start + HD, :].T

    def step(member, carry):
        table = held_ref[member, SLOTS * WIDE :, :].astype(jnp.float32)
        sources = key_members(member, core)
        load = lambda source, start: lambda: held_ref[source, start : start + HD, :]
        turned = lambda source, slot: lambda: key_ref[source, slot]
        items = [
            (load(member, slot * WIDE), turned(source, slot), load(source, slot * WIDE + 2 * HD))
            for slot in range(SLOTS)
            for source in sources
        ]
        results = attend_all(items, score_ref, weight_ref, 1)
        stats = []
        for slot in range(SLOTS):
            at = slot * KEYS
            accum, top, total = merge(
                [results[at + entry] + (table[at + entry : at + entry + 1],) for entry in range(KEYS)]
            )
            back_ref[member, slot * HD : (slot + 1) * HD, :] = (accum / total).astype(jnp.bfloat16)
            stats.extend(thirds(top + jnp.log(total)))
        back_ref[member, SLOTS * HD :, :] = stack_rows(stats, 8, BLOCK).astype(jnp.bfloat16)
        pltpu.make_async_copy(back_ref.at[member], back_hbm.at[member], sems.at[member]).start()
        return carry

    lax.fori_loop(0, HEADS, step, 0)
    for member in range(HEADS):
        pltpu.make_async_copy(back_ref.at[member], back_hbm.at[member], sems.at[member]).wait()


def near_kernel(index_ref, links_ref, chunk_ref, edge_ref, out_ref, score_ref, weight_ref, count):
    index = index_ref[0]
    y = index & 7
    outer = ((y == 0) & (index > 0)) | ((y == Y_COUNT - 1) & (index < count - 1))
    times = [(links_ref[0] >> CORE_BIT) & 1, jnp.where(outer, 1, 0)]
    rows = [jnp.full((1, BLOCK), number, jnp.int32).astype(jnp.float32) for number in times]

    def step(group, carry):
        items = []
        load = lambda ref, head, start: lambda: ref[head, start : start + HD, :]
        for local in range(4):
            head = 4 * group + local
            query = load(chunk_ref, head, 0)
            items.append((query, load(chunk_ref, head, WIDE + HD), load(chunk_ref, head, WIDE + 2 * HD)))
            items.append((query, load(edge_ref, head, 0), load(edge_ref, head, HD)))
        results = attend_all(items, score_ref, weight_ref)
        for local in range(4):
            accum, top, total = merge([results[2 * local + entry] + (rows[entry],) for entry in range(2)])
            head = 4 * group + local
            out_ref[head, :HD, :] = accum
            out_ref[head, HD:, :] = stack_rows([top, total], 8, BLOCK)
        return carry

    lax.fori_loop(0, HEADS // 4, step, 0)


def home_kernel(links_ref, chunk_ref, x_lo_ref, x_hi_ref, near_ref, out_ref, score_ref, weight_ref):
    times = [(links_ref[0] >> bit) & 1 for bit in (3, 5)]
    rows = [jnp.full((1, BLOCK), number, jnp.int32).astype(jnp.float32) for number in times]

    def step(group, carry):
        items = []
        load = lambda ref, head, start: lambda: ref[head, start : start + HD, :]
        for local in range(4):
            head = 4 * group + local
            for ref in (x_lo_ref, x_hi_ref):
                items.append((load(chunk_ref, head, 0), load(ref, head, 0), load(ref, head, HD)))
        results = attend_all(items, score_ref, weight_ref)
        for local in range(4):
            head = 4 * group + local
            near_total = near_ref[head, HD + 1 : HD + 2, :]
            near = (near_ref[head, :HD, :], near_ref[head, HD : HD + 1, :])
            accum, top, total = merge([results[2 * local + entry] + (rows[entry],) for entry in range(2)])
            peak = jnp.maximum(near[1], top)
            near_factor, factor = jnp.exp2((near[1] - peak) * LOG2E), jnp.exp2((top - peak) * LOG2E)
            out_ref[head, :HD, :] = near_factor * near[0] + factor * accum
            out_ref[head, HD:, :] = stack_rows([peak, near_factor * near_total + factor * total], 8, BLOCK)
        return carry

    lax.fori_loop(0, HEADS // 4, step, 0)


def finish_kernel(home_ref, own_ref, other_ref, out_ref):
    for pair in range(HEADS // 2):
        turned = []
        for head in (2 * pair, 2 * pair + 1):
            home_top = home_ref[head, HD : HD + 1, :]
            parts = [(home_ref[head, :HD, :], home_top, home_ref[head, HD + 1 : HD + 2, :])]
            for ref, slot in ((own_ref, 0), (other_ref, 1)):
                value = ref[head, slot * HD : (slot + 1) * HD, :].astype(jnp.float32)
                stats = ref[head, SLOTS * HD :, :].astype(jnp.float32)
                at = 3 * slot
                parts.append((value, stats[at : at + 1] + stats[at + 1 : at + 2] + stats[at + 2 : at + 3], 1.0))
            top = functools.reduce(jnp.maximum, [peak for _, peak, _ in parts])
            factors = [jnp.exp2((peak - top) * LOG2E) for _, peak, _ in parts]
            accum = sum(factor * value for factor, (value, _, _) in zip(factors, parts))
            total = sum(factor * row_sum for factor, (_, _, row_sum) in zip(factors, parts))
            turned.append(accum / total)
        out_ref[:, pair * 2 * HD : (pair + 1) * 2 * HD] = jnp.concatenate(turned, axis=0).T


SMEM = pl.BlockSpec(memory_space=pltpu.SMEM)
WHOLE = pl.BlockSpec(memory_space=pltpu.VMEM)
HBM = pl.BlockSpec(memory_space=pltpu.HBM)


def call(kernel, specs, shapes, scratch, flops, moved, *operands, limit=VMEM_LIMIT, outs=None):
    return pl.pallas_call(
        kernel,
        in_specs=specs,
        out_specs=outs or ([WHOLE] * len(shapes) if isinstance(shapes, list) else WHOLE),
        out_shape=shapes,
        scratch_shapes=scratch,
        compiler_params=pltpu.CompilerParams(vmem_limit_bytes=limit),
        cost_estimate=pl.CostEstimate(flops=flops, bytes_accessed=moved, transcendentals=0),
    )(*operands)


def per_device(tokens, norm_gain, norm_shift, w_qkv, links, count):
    groups = split_groups(count)
    width = w_qkv.shape[0]
    bf16, f32 = jnp.bfloat16, jnp.float32
    index = (lax.axis_index("row") * lax.axis_size("col") + lax.axis_index("col")).astype(jnp.int32)[None]
    attend_scratch = [pltpu.VMEM((2 * KEYS, BLOCK, BLOCK), f32), pltpu.VMEM((2 * KEYS, BLOCK, BLOCK), bf16)]
    normed = call(
        norm_kernel,
        [SMEM] * 2 + [WHOLE] * 2,
        jax.ShapeDtypeStruct((BLOCK + 16, width), bf16),
        [],
        13 * 10**9,
        2**20,
        index,
        links,
        tokens,
        jnp.stack([norm_gain, norm_shift]),
    )
    other = lax.ppermute(normed, AXES, xor_pairs(count, CORE_BIT))
    edge = lax.ppermute(normed, AXES, edge_pairs(count))
    chunks, keyval = call(
        project_kernel,
        [SMEM] * 2 + [WHOLE] * 3,
        [jax.ShapeDtypeStruct((HEADS, CHUNK, BLOCK), bf16), jax.ShapeDtypeStruct((HEADS, 2 * HD, BLOCK), bf16)],
        [
            pltpu.VMEM((2 * BLOCK, width), bf16),
            pltpu.VMEM((HEADS, CHUNK, BLOCK), bf16),
            pltpu.SemaphoreType.DMA((2,)),
        ],
        20 * 2 * 2 * BLOCK * w_qkv.shape[0] * w_qkv.shape[1],
        6 * 2**20,
        index,
        links,
        normed,
        other,
        w_qkv,
        outs=[HBM, WHOLE],
    )
    held = lax.all_to_all(chunks, AXES, 0, 0, axis_index_groups=groups, tiled=True)
    from_edge = call(
        edge_kernel,
        [WHOLE] * 2,
        jax.ShapeDtypeStruct((HEADS, 2 * HD, BLOCK), bf16),
        [],
        30 * 2 * BLOCK * w_qkv.shape[0] * w_qkv.shape[1],
        4 * 2**20,
        edge,
        w_qkv,
    )
    from_x_lo = lax.ppermute(keyval, AXES, xor_pairs(count, 3))
    from_x_hi = lax.ppermute(keyval, AXES, xor_pairs(count, 5))
    near = call(
        functools.partial(near_kernel, count=count),
        [SMEM] * 2 + [WHOLE] * 2,
        jax.ShapeDtypeStruct((HEADS, HD + 8, BLOCK), f32),
        attend_scratch,
        16 * 4 * BLOCK * BLOCK * 256,
        4 * 2**20,
        index,
        links,
        chunks,
        from_edge,
    )
    held, near = lax.optimization_barrier((held, near))
    back = call(
        group_kernel,
        [SMEM, WHOLE],
        jax.ShapeDtypeStruct((HEADS, BACK, BLOCK), bf16),
        attend_scratch
        + [pltpu.VMEM((HEADS, SLOTS, BLOCK, HD), bf16), pltpu.VMEM((HEADS, BACK, BLOCK), bf16), pltpu.SemaphoreType.DMA((HEADS,))],
        20 * 64 * 4 * BLOCK * BLOCK * 256,
        3 * 2**20,
        index,
        held,
        outs=HBM,
    )
    mine = lax.all_to_all(back, AXES, 0, 0, axis_index_groups=groups, tiled=True)
    home = call(
        home_kernel,
        [SMEM] + [WHOLE] * 4,
        jax.ShapeDtypeStruct((HEADS, HD + 8, BLOCK), f32),
        attend_scratch,
        20 * 32 * 4 * BLOCK * BLOCK * 256,
        4 * 2**20,
        links,
        chunks,
        from_x_lo,
        from_x_hi,
        near,
    )
    mine, home = lax.optimization_barrier((mine, home))
    theirs = lax.ppermute(mine, AXES, xor_pairs(count, CORE_BIT))
    return call(
        finish_kernel,
        [WHOLE] * 3,
        jax.ShapeDtypeStruct((BLOCK, INNER), f32),
        [],
        10**7,
        2 * 2**20,
        home,
        mine,
        theirs,
    )


def solution(mesh):
    placed = (P(AXES, None), P(), P(), P(), P(AXES))
    return jax.shard_map(
        functools.partial(per_device, count=mesh.size),
        mesh=mesh,
        in_specs=placed,
        out_specs=P(AXES, None),
        check_vma=False,
    )
```
